32 devices in a mesh: fsdp: 2 (over y), context: 4 (over x, core), tensor: 4 (over z).
Axes of the slice: x: 2, y: 2, z: 4, core: 2. Of those that a mesh axis runs over, the one named last changes fastest.
Arguments:
- tokens: bfloat16 [16, 2048, 960], P('fsdp', ('context', 'tensor')), may hold values from -6 to 6
- gain_attn: bfloat16 [960], P(('fsdp', 'context')), may hold values from 0.5 to 1.5
- w_query: bfloat16 [960, 960], P(('fsdp', 'context')), may hold values from -0.25 to 0.25
- w_key: bfloat16 [960, 320], P(('fsdp', 'context')), may hold values from -0.25 to 0.25
- w_value: bfloat16 [960, 320], P(('fsdp', 'context')), may hold values from -0.1875 to 0.1875
- w_out: bfloat16 [960, 960], P(None, ('fsdp', 'context')), may hold values from -1.25 to 1.25
- gain_mlp: bfloat16 [960], P(('fsdp', 'context')), may hold values from 0.5 to 1.5
- w_gate: bfloat16 [960, 2560], P(('fsdp', 'context'), 'tensor'), may hold values from -0.1875 to 0.1875
- w_up: bfloat16 [960, 2560], P(('fsdp', 'context'), 'tensor'), may hold values from -0.1875 to 0.1875
- w_down: bfloat16 [2560, 960], P('tensor', ('fsdp', 'context')), may hold values from -0.25 to 0.25
- cotangent: bfloat16 [16, 2048, 960], P('fsdp', ('context', 'tensor')), may hold values from -6 to 6
Outputs:
- output: float32 [16, 2048, 960], P('fsdp', ('context', 'tensor'))
- grad_tokens: float32 [16, 2048, 960], P('fsdp', ('context', 'tensor'))
- grad_gain_attn: float32 [960], P(('fsdp', 'context'))
- grad_query: float32 [960, 960], P(('fsdp', 'context'))
- grad_key: float32 [960, 320], P(('fsdp', 'context'))
- grad_value: float32 [960, 320], P(('fsdp', 'context'))
- grad_out: float32 [960, 960], P(None, ('fsdp', 'context'))
- grad_gain_mlp: float32 [960], P(('fsdp', 'context'))
- grad_gate: float32 [960, 2560], P(('fsdp', 'context'), 'tensor')
- grad_up: float32 [960, 2560], P(('fsdp', 'context'), 'tensor')
- grad_down: float32 [2560, 960], P('tensor', ('fsdp', 'context'))
The draws below stay inside these ranges and needn't reach their ends.
All inputs are finite; a program needn't handle non-finite values.
Results may differ from the reference program's by a relative error of at most 0.018.
Values may be sent and summed in bfloat16 or wider, within the bound.
A program may use at most 256 MiB of HBM per device.

```python
import math
import jax
import jax.numpy as jnp
from jax import lax

D = 960
HEADS = 15
KV_HEADS = 5
HEAD_DIM = 64
FF = 2560
SEQ_LEN = 2048
BATCH = 16


def spiked(array, key, source, target, shards_of, factor):
    owner, partner = [(jnp.arange(array.shape[axis_at]) // (array.shape[axis_at] // shards_of)).reshape([-1 if axis == axis_at else 1 for axis in range(array.ndim)]) for axis_at in (source, target)]
    chosen = jax.random.permutation(key, shards_of)[partner]
    strong = (owner == chosen) | (owner == (partner + shards_of // 2) % shards_of)
    return jnp.where(strong, factor * array, array)


def level_of(stream_key, extent, shards, low, high):
    gain = 1.0
    for axis_at, blocks in shards:
        heights = jax.random.uniform(jax.random.fold_in(jax.random.fold_in(stream_key, 6), axis_at), (blocks,), jnp.float32, low / len(shards), high / len(shards))
        gain = gain * jnp.repeat(jnp.exp(heights), extent[axis_at] // blocks).reshape((-1,) + (1,) * (len(extent) - 1 - axis_at))
    return gain


def noise(rng, dims, deviation, most, cuts=(), dtype=jnp.bfloat16):
    array = jax.random.normal(rng, dims, jnp.float32) * deviation
    if len(cuts) > 0:
        array = level_of(rng, dims, cuts, -0.22, 0.18) * array
    return jnp.clip(array, min=-most, max=most).astype(dtype)


def noise_with(stream_key, shape, spread, limit, pieces, heavy, held_as=jnp.bfloat16):
    entries = spread * jax.random.normal(stream_key, shape, jnp.float32)
    if pieces:
        entries = entries * level_of(stream_key, shape, pieces, -0.22, 0.18)
    return jnp.clip(spiked(entries, jax.random.fold_in(stream_key, 3), *heavy), -limit, limit).astype(held_as)


def setup_inputs(seed: int = 0) -> dict:
    arg_keys = jax.random.split(jax.random.key(seed), 12)
    return {
        "tokens": noise(arg_keys[0], (BATCH, SEQ_LEN, D), 1.0, 6.0, ((0, 2), (1, 16))),
        "gain_attn": jnp.clip(1.0 + 0.1 * jax.random.normal(arg_keys[1], (D,), jnp.float32), 0.5, 1.5).astype(jnp.bfloat16),
        "w_query": noise(arg_keys[2], (D, HEADS * HEAD_DIM), (D // 2) ** -0.5, 0.25, ((0, 8),)),
        "w_key": noise(arg_keys[3], (D, KV_HEADS * HEAD_DIM), (D // 2) ** -0.5, 0.25, ((0, 8),)),
        "w_value": noise(arg_keys[4], (D, KV_HEADS * HEAD_DIM), D ** -0.5, 0.1875, ((0, 8),)),
        "w_out": noise(arg_keys[5], (HEADS * HEAD_DIM, D), (max(D // 48, 1)) ** -0.5, 1.25, ((1, 8),)),
        "gain_mlp": jnp.clip(1.0 + 0.1 * jax.random.normal(arg_keys[6], (D,), jnp.float32), 0.5, 1.5).astype(jnp.bfloat16),
        "w_gate": noise(arg_keys[7], (D, FF), D ** -0.5, 0.1875, ((0, 8), (1, 4))),
        "w_up": noise(arg_keys[8], (D, FF), D ** -0.5, 0.1875, ((0, 8), (1, 4))),
        "w_down": noise(arg_keys[9], (FF, D), (FF // 4) ** -0.5, 0.25, ((0, 4), (1, 8))),
        "cotangent": noise_with(arg_keys[10], (BATCH, SEQ_LEN, D), 1.0, 6.0, ((0, 2), (1, 16)), (0, 2, 2, 2.0)),
    }


@jax.custom_vjp
def low(v):
    return lax.optimization_barrier(v.astype(jnp.bfloat16)).astype(jnp.float32)

@jax.custom_vjp
def low_back(v):
    return v

def low_keep(v):
    return (low(v), None)

def low_pass(kept, grad):
    return (grad,)

def back_keep(v):
    return (v, None)

def back_low(kept, grad):
    return (low(grad),)
low.defvjp(low_keep, low_pass)
low_back.defvjp(back_keep, back_low)
epsilon = 1e-05
rope_base = 10000.0
neg_large = -1e+30
highest = lax.Precision.HIGHEST

def normed(values, gain_vec):
    inv_rms = lax.rsqrt(lax.optimization_barrier(jnp.mean(values * values, axis=-1, keepdims=True)) + epsilon)
    return values * inv_rms * gain_vec

def tables(positions):
    step_index = jnp.arange(HEAD_DIM // 2).astype(jnp.float32)
    frequency = jnp.power(rope_base, -2.0 * step_index / HEAD_DIM)
    angles = positions.astype(jnp.float32)[:, None] * frequency[None, :]
    return (jnp.cos(angles), jnp.sin(angles))

def rotate(values, cos_t, sin_t):
    half_dim = values.shape[-1] // 2
    first_half = values[..., :half_dim]
    second_half = values[..., half_dim:]
    return jnp.concatenate([first_half * cos_t - second_half * sin_t, second_half * cos_t + first_half * sin_t], axis=-1)

def attend(queries, key_rows, value_rows):
    length = queries.shape[0]
    block_len = math.gcd(length, 512)
    group_size = HEADS // KV_HEADS
    blocks = queries.reshape(length // block_len, block_len, KV_HEADS, group_size, HEAD_DIM)
    starts = (jnp.arange(length // block_len) * block_len).astype(jnp.int32)
    key_index = jnp.arange(length)
    inv_root = 1.0 / math.sqrt(HEAD_DIM)

    def one_block(block_args):
        query_rows, first_row = block_args
        scores = jnp.einsum('qhgd,khd->hgqk', query_rows, key_rows, precision=highest) * inv_root
        scores = low_back(scores)
        allowed = key_index[None, :] <= (first_row + jnp.arange(block_len))[:, None]
        scores = jnp.where(allowed, scores, neg_large)
        row_top = lax.optimization_barrier(jnp.max(scores, axis=-1, keepdims=True))
        weights = jnp.exp(scores - row_top)
        weights = weights / lax.optimization_barrier(jnp.sum(weights, axis=-1, keepdims=True))
        weights = low(weights)
        mixed = jnp.einsum('hgqk,khd->qhgd', weights, value_rows, precision=highest)
        return mixed.reshape(block_len, HEADS * HEAD_DIM)
    return lax.map(jax.checkpoint(one_block), (blocks, starts)).reshape(length, HEADS * HEAD_DIM)

def one_layer(tokens, gain_attn, w_query, w_key, w_value, w_out, gain_mlp, w_gate, w_up, w_down):
    length = tokens.shape[0]
    normed_attn = low(normed(tokens, gain_attn))
    queries = low_back(jnp.dot(normed_attn, w_query, precision=highest)).reshape(length, HEADS, HEAD_DIM)
    key_rows = low_back(jnp.dot(normed_attn, w_key, precision=highest)).reshape(length, KV_HEADS, HEAD_DIM)
    value_rows = low(low_back(jnp.dot(normed_attn, w_value, precision=highest))).reshape(length, KV_HEADS, HEAD_DIM)
    cos_t, sin_t = tables(jnp.arange(length))
    queries = low(rotate(queries, cos_t[:, None, :], sin_t[:, None, :]))
    key_rows = low(rotate(key_rows, cos_t[:, None, :], sin_t[:, None, :]))
    heads_out = low(low_back(attend(queries, key_rows, value_rows)))
    middle = tokens + low_back(jnp.dot(heads_out, w_out, precision=highest))
    normed_mlp = low(normed(middle, gain_mlp))
    gate_pre = low_back(jnp.dot(normed_mlp, w_gate, precision=highest))
    up_pre = low_back(jnp.dot(normed_mlp, w_up, precision=highest))
    hidden = low(jax.nn.silu(gate_pre) * up_pre)
    return middle + jnp.dot(hidden, w_down, precision=highest)

def reference(tokens, gain_attn, w_query, w_key, w_value, w_out, gain_mlp, w_gate, w_up, w_down, cotangent):
    weights = tuple((w_item.astype(jnp.float32) for w_item in (gain_attn, w_query, w_key, w_value, w_out, gain_mlp, w_gate, w_up, w_down)))
    inputs = tokens.astype(jnp.float32)
    cot_all = cotangent.astype(jnp.float32)

    def step_seq(totals, seq_pair):
        one_seq, seq_cot = seq_pair
        layer_out, pull_back = jax.vjp(one_layer, one_seq, *weights)
        seq_grads = pull_back(seq_cot)
        return (tuple((acc_item + new_item for acc_item, new_item in zip(totals, seq_grads[1:]))), (layer_out, seq_grads[0]))
    start_sums = tuple((jnp.zeros(w_item.shape, jnp.float32) for w_item in weights))
    totals, (outputs, grad_in) = lax.scan(step_seq, start_sums, (inputs, cot_all))
    return (outputs, grad_in, totals[0], totals[1], totals[2], totals[3], totals[4], totals[5], totals[6], totals[7], totals[8])
```

```python
import math

import jax
import jax.numpy as jnp
from jax import lax
from jax.experimental import pallas as pl
from jax.experimental.pallas import tpu as pltpu
from jax.sharding import PartitionSpec as P

HEADS = 15
KV_HEADS = 5
HEAD_DIM = 64


epsilon = 1e-05
rope_base = 10000.0
neg_large = -1e30


def rms_scale(values):
    return lax.rsqrt(jnp.mean(values * values, axis=-1, keepdims=True) + epsilon)


def tables(positions):
    step_index = jnp.arange(HEAD_DIM // 2).astype(jnp.float32)
    frequency = jnp.power(rope_base, -2.0 * step_index / HEAD_DIM)
    angles = positions.astype(jnp.float32)[:, None] * frequency[None, :]
    return (jnp.cos(angles), jnp.sin(angles))


def rotate(values, cos_t, sin_t):
    half_dim = values.shape[-1] // 2
    first_half = values[..., :half_dim]
    second_half = values[..., half_dim:]
    return jnp.concatenate(
        [first_half * cos_t - second_half * sin_t, second_half * cos_t + first_half * sin_t],
        axis=-1,
    )


def contract_rows(left_mat, right_mat):
    return lax.dot_general(
        left_mat, right_mat, (((0,), (0,)), ((), ())), preferred_element_type=jnp.float32
    )


def contract_cols(left_mat, right_mat):
    return lax.dot_general(
        left_mat, right_mat, (((1,), (1,)), ((), ())), preferred_element_type=jnp.float32
    )


def bits_of(axis_name):
    return [1 << k for k in range(int(math.log2(lax.axis_size(axis_name))))]


def swap(values, axis_name, bit):
    size = lax.axis_size(axis_name)
    return lax.ppermute(values, axis_name, [(i, i ^ bit) for i in range(size)])


def reduce_rows(partial, order):
    fsdp, context = (lax.axis_size("fsdp"), lax.axis_size("context"))
    names = [("fsdp", b) for b in reversed(bits_of("fsdp"))]
    names += [("context", b) for b in reversed(bits_of("context"))]
    rows, columns = partial.shape
    block = partial.astype(jnp.bfloat16).reshape(
        (2,) * len(names) + (rows // (fsdp * context), columns)
    )
    for step in order:
        dim = names.index(step)
        names.pop(dim)
        axis_name, bit = step
        mine = (lax.axis_index(axis_name) // bit) % 2
        sent = lax.dynamic_index_in_dim(block, 1 - mine, dim, keepdims=False)
        kept = lax.dynamic_index_in_dim(block, mine, dim, keepdims=False)
        arrived = swap(sent, axis_name, bit)
        block = (kept.astype(jnp.float32) + arrived.astype(jnp.float32)).astype(jnp.bfloat16)
    return block


def orders():
    core = [("context", b) for b in bits_of("context")[:1]]
    chips = [("context", b) for b in bits_of("context")[1:]]
    outer = [("fsdp", b) for b in bits_of("fsdp")]
    return (core + chips + outer, core + outer + chips)


def reduce_units(block):
    rows, columns = block.shape
    size = lax.axis_size("tensor")
    parts = jnp.transpose(block.reshape(rows, size, columns // size), (1, 0, 2))
    for bit in bits_of("tensor"):
        mine = (lax.axis_index("tensor") // bit) % 2
        pairs = parts.reshape((parts.shape[0] // 2, 2) + parts.shape[1:])
        sent = lax.dynamic_index_in_dim(pairs, 1 - mine, 1, keepdims=False)
        kept = lax.dynamic_index_in_dim(pairs, mine, 1, keepdims=False)
        arrived = swap(sent, "tensor", bit)
        total = kept.astype(jnp.float32) + arrived.astype(jnp.float32)
        parts = total.astype(jnp.bfloat16)
    return total.reshape(rows, columns // size)


def reduce_copies(block):
    for bit in bits_of("tensor"):
        arrived = swap(block, "tensor", bit)
        total = block.astype(jnp.float32) + arrived.astype(jnp.float32)
        block = total.astype(jnp.bfloat16)
    return total


def to_sequences(rows):
    context = lax.axis_size("context")
    seqs, count, width = rows.shape
    parts = rows.reshape(context, seqs // context, count, width)
    moved = lax.all_to_all(parts, "context", 0, 0, tiled=False)
    return jnp.transpose(moved, (1, 0, 2, 3))


def to_positions(rows):
    context = lax.axis_size("context")
    seqs, blocks, count, width = rows.shape
    parts = jnp.transpose(rows, (1, 0, 2, 3))
    moved = lax.all_to_all(parts, "context", 0, 0, tiled=False)
    return moved.reshape(context * seqs, count, width)


def dot32(left_mat, right_mat):
    return jnp.dot(left_mat, right_mat, preferred_element_type=jnp.float32)


def attend_kernel(span, q_t_ref, key_ref, v_t_ref, bias_ref, out_ref, log_ref):
    chunk = pl.program_id(1)
    q_t = q_t_ref[0, 0]
    columns = q_t.shape[1]

    def one_block(block_index, state, bias):
        top_run, sum_run, acc_run = state
        rows = pl.ds(pl.multiple_of(block_index * span, span), span)
        scores = dot32(key_ref[0, rows, :], q_t)
        if bias is not None:
            scores = scores + bias
        top_new = jnp.maximum(top_run, jnp.max(scores, axis=0, keepdims=True))
        expo = jnp.exp(scores - top_new)
        shrink = jnp.exp(top_run - top_new)
        sum_new = sum_run * shrink + jnp.sum(expo, axis=0, keepdims=True)
        mixed = dot32(v_t_ref[0, block_index], expo.astype(jnp.bfloat16))
        return (top_new, sum_new, acc_run * shrink + mixed)

    state = (
        jnp.full((1, columns), neg_large, jnp.float32),
        jnp.zeros((1, columns), jnp.float32),
        jnp.zeros((HEAD_DIM, columns), jnp.float32),
    )
    state = one_block(chunk, state, bias_ref[...])
    top, total, acc = lax.fori_loop(0, chunk, lambda j, s: one_block(j, s, None), state)
    out_ref[0, 0] = acc / total
    log_ref[0, 0] = top + jnp.log(total)


def back_kernel(
    span,
    q_ref,
    q_t_ref,
    do_ref,
    do_t_ref,
    out_ref,
    log_ref,
    key_ref,
    k_t_ref,
    value_ref,
    bias_ref,
    dq_ref,
    dk_ref,
    dv_ref,
):
    chunk = pl.program_id(1)

    @pl.when(chunk == 0)
    def _():
        dk_ref[...] = jnp.zeros_like(dk_ref)
        dv_ref[...] = jnp.zeros_like(dv_ref)

    queries = q_ref[0, 0]
    q_t = q_t_ref[0, 0]
    d_out = do_ref[0, 0]
    d_out_t = do_t_ref[0, 0]
    log_sum = log_ref[0, 0]
    delta = jnp.sum(d_out_t.astype(jnp.float32) * out_ref[0, 0], axis=0, keepdims=True)

    def one_block(block_index, dq_acc, bias):
        rows = pl.ds(pl.multiple_of(block_index * span, span), span)
        scores = dot32(key_ref[0, rows, :], q_t)
        if bias is not None:
            scores = scores + bias
        probs = jnp.exp(scores - log_sum)
        d_probs = dot32(value_ref[0, rows, :], d_out_t)
        d_scores = (probs * (d_probs - delta)).astype(jnp.bfloat16)
        dv_ref[0, rows, :] += dot32(probs.astype(jnp.bfloat16), d_out)
        dk_ref[0, rows, :] += dot32(d_scores, queries)
        return dq_acc + dot32(k_t_ref[0, block_index], d_scores)

    dq_acc = one_block(chunk, jnp.zeros(q_t.shape, jnp.float32), bias_ref[...])
    dq_acc = lax.fori_loop(0, chunk, lambda j, s: one_block(j, s, None), dq_acc)
    dq_ref[0, 0] = dq_acc * (1.0 / math.sqrt(HEAD_DIM))


def per_chunk(*shape):
    return pl.BlockSpec((1, 1) + shape, lambda h, c: (h, c, 0, 0))


def per_head(*shape):
    return pl.BlockSpec((1,) + shape, lambda h, c: (h,) + (0,) * len(shape))


def whole(*shape):
    return pl.BlockSpec(shape, lambda h, c: (0,) * len(shape))


def attend(q_t, keys, v_t, bias):
    heads, chunks, dim, columns = q_t.shape
    span = bias.shape[0]
    length = keys.shape[1]
    pairs = heads * columns * span * chunks * (chunks + 1) // 2
    return pl.pallas_call(
        lambda *refs: attend_kernel(span, *refs),
        grid=(heads, chunks),
        in_specs=[
            per_chunk(dim, columns),
            per_head(length, dim),
            per_head(chunks, dim, span),
            whole(span, columns),
        ],
        out_specs=[per_chunk(dim, columns), per_chunk(1, columns)],
        out_shape=[
            jax.ShapeDtypeStruct((heads, chunks, dim, columns), jnp.float32),
            jax.ShapeDtypeStruct((heads, chunks, 1, columns), jnp.float32),
        ],
        cost_estimate=pl.CostEstimate(
            flops=16 * dim * pairs, bytes_accessed=8 * q_t.size, transcendentals=pairs
        ),
        compiler_params=pltpu.CompilerParams(vmem_limit_bytes=40 * 1024 * 1024),
        name="attend",
    )(q_t, keys, v_t, bias)


def attend_back(queries, q_t, d_out, d_out_t, out, log_sum, keys, k_t, values, bias):
    heads, chunks, dim, columns = q_t.shape
    span = bias.shape[0]
    length = keys.shape[1]
    pairs = heads * columns * span * chunks * (chunks + 1) // 2
    return pl.pallas_call(
        lambda *refs: back_kernel(span, *refs),
        grid=(heads, chunks),
        in_specs=[
            per_chunk(columns, dim),
            per_chunk(dim, columns),
            per_chunk(columns, dim),
            per_chunk(dim, columns),
            per_chunk(dim, columns),
            per_chunk(1, columns),
            per_head(length, dim),
            per_head(chunks, dim, span),
            per_head(length, dim),
            whole(span, columns),
        ],
        out_specs=[per_chunk(dim, columns), per_head(length, dim), per_head(length, dim)],
        out_shape=[
            jax.ShapeDtypeStruct((heads, chunks, dim, columns), jnp.float32),
            jax.ShapeDtypeStruct((heads, length, dim), jnp.float32),
            jax.ShapeDtypeStruct((heads, length, dim), jnp.float32),
        ],
        cost_estimate=pl.CostEstimate(
            flops=40 * dim * pairs, bytes_accessed=16 * q_t.size, transcendentals=pairs
        ),
        compiler_params=pltpu.CompilerParams(vmem_limit_bytes=40 * 1024 * 1024),
        name="attend_back",
    )(queries, q_t, d_out, d_out_t, out, log_sum, keys, k_t, values, bias)


def body(
    tokens, gain_attn, w_query, w_key, w_value, w_out, gain_mlp, w_gate, w_up, w_down, cotangent
):
    seq_count, row_count, model_width = tokens.shape
    group_size = HEADS // KV_HEADS
    kv_width = KV_HEADS * HEAD_DIM
    q_width = HEADS * HEAD_DIM
    inv_root = 1.0 / math.sqrt(HEAD_DIM)
    rows_axes = ("fsdp", "context")
    chunks = lax.axis_size("context")
    turns = lax.axis_size("tensor")
    seqs = seq_count // chunks
    own_rows = w_query.shape[0]
    gains = jnp.stack([gain_attn, gain_mlp] + [jnp.zeros_like(gain_attn)] * 126, axis=1)
    attn_pack = jnp.concatenate([w_query, w_key, w_value, w_out.T, gains], axis=1)
    attn_all = lax.all_gather(attn_pack, rows_axes, axis=0, tiled=True)
    in_seq = to_sequences(tokens)
    mlp_pack = jnp.stack([w_gate, w_up, w_down.T])
    mlp_all = lax.all_gather(mlp_pack, ("fsdp", "context", "tensor"), axis=0, tiled=False)
    cot_seq = to_sequences(cotangent)
    w_qkv = attn_all[:, : q_width + 2 * kv_width]
    w_out_t = attn_all[:, q_width + 2 * kv_width : 2 * q_width + 2 * kv_width]
    gain_columns = attn_all[:, 2 * q_width + 2 * kv_width :].astype(jnp.float32)
    g_attn = gain_columns[:, 0]
    g_mlp = gain_columns[:, 1]

    block_start = lax.axis_index("tensor") * row_count
    span = turns * row_count
    positions = (
        jnp.arange(chunks)[:, None] * span + block_start + jnp.arange(row_count)[None, :]
    ).reshape(-1)
    cos_t, sin_t = tables(positions)
    cos_b = cos_t[:, None, :]
    sin_b = sin_t[:, None, :]
    local_rows = chunks * row_count
    query_place = jnp.tile(block_start + jnp.arange(row_count), group_size)
    bias = jnp.where(jnp.arange(span)[:, None] <= query_place[None, :], 0.0, neg_large)
    bias = bias.astype(jnp.float32)

    inputs = in_seq.reshape(seqs, local_rows, model_width).astype(jnp.float32)
    rms_attn = rms_scale(inputs)
    flat_attn = (inputs * rms_attn * g_attn).astype(jnp.bfloat16).reshape(-1, model_width)
    qkv = dot32(flat_attn, w_qkv).reshape(seqs, local_rows, HEADS + 2 * KV_HEADS, HEAD_DIM)
    turned = rotate(qkv[:, :, : HEADS + KV_HEADS], cos_b, sin_b)
    queries = (turned[:, :, :HEADS] * inv_root).astype(jnp.bfloat16)
    key_value = jnp.concatenate(
        [turned[:, :, HEADS:].astype(jnp.bfloat16), qkv[:, :, HEADS + KV_HEADS :].astype(jnp.bfloat16)],
        axis=2,
    ).reshape(seqs, chunks, row_count, 2 * kv_width)

    def rows_major(part):
        parts = part.reshape(chunks, row_count, KV_HEADS, group_size, HEAD_DIM)
        return jnp.transpose(parts, (2, 0, 3, 1, 4)).reshape(
            KV_HEADS, chunks, group_size * row_count, HEAD_DIM
        )

    def columns_major(part):
        parts = part.reshape(chunks, row_count, KV_HEADS, group_size, HEAD_DIM)
        return jnp.transpose(parts, (2, 0, 4, 3, 1)).reshape(
            KV_HEADS, chunks, HEAD_DIM, group_size * row_count
        )

    def from_columns(part):
        parts = part.reshape(KV_HEADS, chunks, HEAD_DIM, group_size, row_count)
        return jnp.transpose(parts, (1, 4, 0, 3, 2)).reshape(local_rows, HEADS, HEAD_DIM)

    saved = []
    heads_list = []
    for seq in range(seqs):
        gathered = lax.all_gather(key_value[seq], "tensor", axis=0, tiled=False)
        kv = gathered.reshape(turns, chunks, row_count, 2, KV_HEADS, HEAD_DIM)
        kv_rows = jnp.transpose(kv, (3, 4, 1, 0, 2, 5)).reshape(
            2, KV_HEADS, chunks * span, HEAD_DIM
        )
        kv_cols = jnp.transpose(kv, (3, 4, 1, 5, 0, 2)).reshape(
            2, KV_HEADS, chunks, HEAD_DIM, span
        )
        q_t = columns_major(queries[seq])
        out, log_sum = attend(q_t, kv_rows[0], kv_cols[1], bias)
        saved.append((q_t, out, log_sum, kv_rows, kv_cols))
        heads_list.append(from_columns(out.astype(jnp.bfloat16)))
    flat_heads = jnp.stack(heads_list).reshape(-1, q_width)

    branch = contract_cols(flat_heads, w_out_t).reshape(seqs, local_rows, model_width)
    middle = inputs + branch
    rms_mlp = rms_scale(middle)
    flat_mlp = (middle * rms_mlp * g_mlp).astype(jnp.bfloat16).reshape(-1, model_width)
    units = w_gate.shape[1]
    mlp_use = jnp.transpose(
        mlp_all.reshape(model_width // own_rows, turns, 3, own_rows, units), (2, 0, 3, 1, 4)
    ).reshape(3, model_width, turns * units)
    w_gate_use, w_up_use, w_down_t = (mlp_use[0], mlp_use[1], mlp_use[2])
    gate_pre = dot32(flat_mlp, w_gate_use)
    up_pre = dot32(flat_mlp, w_up_use)
    sigma_gate = jax.nn.sigmoid(gate_pre)
    silu_gate = gate_pre * sigma_gate
    hidden = (silu_gate * up_pre).astype(jnp.bfloat16)
    result = middle + contract_cols(hidden, w_down_t).reshape(seqs, local_rows, model_width)
    result_out = to_positions(
        result.astype(jnp.bfloat16).reshape(seqs, chunks, row_count, model_width)
    ).astype(jnp.float32)

    flat_grad = cot_seq.reshape(-1, model_width)
    d_hidden = dot32(flat_grad, w_down_t)
    d_gate = (d_hidden * up_pre * sigma_gate * (1.0 + gate_pre * (1.0 - sigma_gate))).astype(
        jnp.bfloat16
    )
    d_up = (d_hidden * silu_gate).astype(jnp.bfloat16)
    first_order, second_order = orders()
    d_normed = contract_cols(d_gate, w_gate_use) + contract_cols(d_up, w_up_use)
    d_normed = d_normed.reshape(seqs, local_rows, model_width)
    grad_down = reduce_units(reduce_rows(contract_rows(flat_grad, hidden), first_order)).T
    grad_gate = reduce_units(reduce_rows(contract_rows(flat_mlp, d_gate), second_order))
    grad_up = reduce_units(reduce_rows(contract_rows(flat_mlp, d_up), first_order))

    norm_mid = middle * rms_mlp
    scaled_mid = d_normed * g_mlp
    gain_mlp_part = jnp.sum(d_normed * norm_mid, axis=(0, 1))
    d_middle = cot_seq.reshape(seqs, local_rows, model_width).astype(jnp.float32) + rms_mlp * (
        scaled_mid - norm_mid * jnp.mean(scaled_mid * norm_mid, axis=-1, keepdims=True)
    )
    d_branch = d_middle.astype(jnp.bfloat16).reshape(-1, model_width)
    grad_out = reduce_copies(reduce_rows(contract_rows(d_branch, flat_heads), second_order)).T
    d_heads = dot32(d_branch, w_out_t).astype(jnp.bfloat16).reshape(seqs, local_rows, q_width)

    dq_list, dkv_list = ([], [])
    for seq in range(seqs):
        q_t, out, log_sum, kv_rows, kv_cols = saved[seq]
        dq, dk, dv = attend_back(
            rows_major(queries[seq]),
            q_t,
            rows_major(d_heads[seq]),
            columns_major(d_heads[seq]),
            out,
            log_sum,
            kv_rows[0],
            kv_cols[0],
            kv_rows[1],
            bias,
        )
        dq_list.append(from_columns(dq))
        dkv = jnp.stack([dk, dv]).astype(jnp.bfloat16)
        dkv = dkv.reshape(2 * KV_HEADS, chunks, turns, row_count, HEAD_DIM)
        dkv = jnp.transpose(dkv, (2, 1, 3, 0, 4)).reshape(turns, local_rows, 2 * kv_width)
        own = lax.psum_scatter(dkv, "tensor", scatter_dimension=0, tiled=False)
        dkv_list.append(own.reshape(local_rows, 2 * KV_HEADS, HEAD_DIM))
    d_query = jnp.stack(dq_list)
    d_kv = jnp.stack(dkv_list).astype(jnp.float32)
    d_query_lin = rotate(d_query, cos_b, -sin_b).astype(jnp.bfloat16)
    d_key_lin = rotate(d_kv[:, :, :KV_HEADS], cos_b, -sin_b).astype(jnp.bfloat16)
    d_value_lin = d_kv[:, :, KV_HEADS:].astype(jnp.bfloat16)
    d_q_flat = d_query_lin.reshape(-1, q_width)
    d_kv_flat = jnp.concatenate([d_key_lin, d_value_lin], axis=2).reshape(-1, 2 * kv_width)
    d_normed_attn = contract_cols(d_q_flat, w_qkv[:, :q_width]) + contract_cols(
        d_kv_flat, w_qkv[:, q_width:]
    )
    d_normed_attn = d_normed_attn.reshape(seqs, local_rows, model_width)
    grad_query = reduce_copies(reduce_rows(contract_rows(flat_attn, d_q_flat), first_order))
    grad_kv = reduce_copies(reduce_rows(contract_rows(flat_attn, d_kv_flat), second_order))
    norm_in = inputs * rms_attn
    scaled_in = d_normed_attn * g_attn
    gain_attn_part = jnp.sum(d_normed_attn * norm_in, axis=(0, 1))
    grad_tokens = d_middle + rms_attn * (
        scaled_in - norm_in * jnp.mean(scaled_in * norm_in, axis=-1, keepdims=True)
    )
    grad_tokens_out = to_positions(
        grad_tokens.astype(jnp.bfloat16).reshape(seqs, chunks, row_count, model_width)
    ).astype(jnp.float32)
    gain_sums = lax.psum(
        jnp.stack([gain_attn_part, gain_mlp_part]), ("fsdp", "context", "tensor")
    )
    own_gains = lax.dynamic_slice_in_dim(
        gain_sums, lax.axis_index(rows_axes) * own_rows, own_rows, 1
    )
    return (
        result_out,
        grad_tokens_out,
        own_gains[0],
        grad_query,
        grad_kv[:, :kv_width],
        grad_kv[:, kv_width:],
        grad_out,
        own_gains[1],
        grad_gate,
        grad_up,
        grad_down,
    )


def solution(mesh):
    placed = (
        P("fsdp", ("context", "tensor"), None),
        P(("fsdp", "context")),
        P(("fsdp", "context"), None),
        P(("fsdp", "context"), None),
        P(("fsdp", "context"), None),
        P(None, ("fsdp", "context")),
        P(("fsdp", "context")),
        P(("fsdp", "context"), "tensor"),
        P(("fsdp", "context"), "tensor"),
        P("tensor", ("fsdp", "context")),
        P("fsdp", ("context", "tensor"), None),
    )
    return jax.shard_map(
        body,
        mesh=mesh,
        in_specs=placed,
        out_specs=(
            P("fsdp", ("context", "tensor"), None),
            P("fsdp", ("context", "tensor"), None),
            P(("fsdp", "context")),
            P(("fsdp", "context"), None),
            P(("fsdp", "context"), None),
            P(("fsdp", "context"), None),
            P(None, ("fsdp", "context")),
            P(("fsdp", "context")),
            P(("fsdp", "context"), "tensor"),
            P(("fsdp", "context"), "tensor"),
            P("tensor", ("fsdp", "context")),
        ),
        check_vma=False,
    )
```
